32 devices in a mesh: groups: 2 (over y), att: 16 (over z, x, core), exp: 1.
Axes of the slice: x: 2, y: 2, z: 4, core: 2. Of those that a mesh axis runs over, the one named last changes fastest.
Arguments:
- queries: bfloat16 [1024, 4096], P(('groups', 'att'), 'exp'), parts along dimension 0, may hold values from -40 to 40
- key_cache: bfloat16 [1024, 2, 256, 128], P(('groups', 'att'), 'exp'), parts along dimension 0, may hold values from -12 to 12
- value_cache: bfloat16 [1024, 2, 256, 128], P(('groups', 'att'), 'exp'), parts along dimension 0, may hold values from -6 to 6
- new_key: bfloat16 [1024, 256], P(('groups', 'att'), 'exp'), parts along dimension 0, may hold values from -6 to 6
- new_value: bfloat16 [1024, 256], P(('groups', 'att'), 'exp'), parts along dimension 0, may hold values from -6 to 6
- lengths: int32 [1024], P(('groups', 'att')), parts along dimension 0, may hold values from 2 to 256, as said below
- residual: bfloat16 [1024, 4096], P(('groups', 'att'), 'exp'), parts along dimension 0, may hold values from -40 to 40
- norm_gain: bfloat16 [4096], P('exp'), may hold values from 0.099609375 to 1.8984375
- expert_ids: int32 [1024, 8], P(('groups', 'att')), parts along dimension 0, may hold values from 0 to 15, all different within a row; in each aligned block of 32 rows (0 to 31, 32 to 63, ...) at most 32 rows name the same one
- gate_probs: float32 [1024, 8], P(('groups', 'att')), parts along dimension 0, may hold values from 0.1 to 1
- gate_proj: bfloat16 [16, 4096, 768], P('att', None, 'exp'), may hold values from -0.09375 to 0.09375
- up_proj: bfloat16 [16, 4096, 768], P('att', None, 'exp'), may hold values from -0.09375 to 0.09375
- down_proj: bfloat16 [16, 768, 4096], P('att', 'exp'), may hold values from -0.21875 to 0.21875
Outputs:
- layer_out: bfloat16 [1024, 4096], P(('groups', 'att'), 'exp'), parts along dimension 0
The draws below stay inside these ranges and needn't reach their ends.
There are 2 independent parts, one for each index of `groups`. The reference program is written for one: setup_inputs(seed, part) draws one part's arguments, and reference() takes and returns one part's arrays. A program takes and returns all parts, laid end to end along the dimension named above; an argument that names none is the same for every part. Nothing has to cross between parts.
Inputs may be any that keep to these rules, and one draw needn't show every extreme that they name: `lengths`: position 0 and 1 of every row are live; some row of every draw has all 256 slots live. `expert_ids`: the 8 experts of a row differ. Among the rows of one index of att (aligned blocks of 32 rows) no expert is named more than 32 times, a bound that some block reaches.
All inputs are finite; a program needn't handle non-finite values.
Results may differ from the reference program's by a relative error of at most 0.0051.
Values may be sent and summed in bfloat16 or wider, within the bound.
A program may use at most 128 MiB of HBM per device.

```python
import math
import jax
import jax.numpy as jnp
import numpy as np
from jax import lax

D = 4096
HD = 128
QH = 32
KVH = 2
FFE = 768
TOPK = 8
ROWS = 32
L = 256
EXPERTS = 16
CAP = 32
TOTAL = 512
N_ATT = 16


def draw_queries(key, part):
    key = jax.random.fold_in(key, 1)
    total_rows = ROWS * N_ATT
    values = jnp.clip(jax.random.normal(key, (total_rows, QH, HD), jnp.float32), -4.0, 4.0)
    return values.reshape(total_rows, QH * HD).astype(jnp.bfloat16)


def draw_key_cache(key, part):
    key = jax.random.fold_in(key, 2)
    shape_all = (ROWS * N_ATT, KVH, L, HD)
    values = jnp.clip(jax.random.normal(key, shape_all, jnp.float32), -4.0, 4.0)
    return values.astype(jnp.bfloat16)


def draw_lengths(key, part):
    key = jax.random.fold_in(key, 3)
    total_rows = ROWS * N_ATT
    drawn = jax.random.randint(key, (total_rows,), 2, L + 1)
    longest = jax.random.randint(jax.random.fold_in(key, 5), (), 0, total_rows)
    return jnp.where(jnp.arange(total_rows) == longest, L, drawn).astype(jnp.int32)


def draw_residual(key, part):
    key = jax.random.fold_in(key, 4)
    total_rows = ROWS * N_ATT
    column = jnp.power(10.0, jnp.linspace(-0.5, 0.5, D)).astype(jnp.float32)
    row_key = jax.random.fold_in(key, 6)
    row_scale = jnp.exp(jax.random.uniform(row_key, (total_rows, 1), jnp.float32, jnp.log(0.3), jnp.log(3.0)))
    entries = jnp.clip(jax.random.normal(key, (total_rows, D), jnp.float32), -4.0, 4.0)
    return (entries * row_scale * column[None, :]).astype(jnp.bfloat16)


def shard_levels(rng, shape, pieces, least, high):
    level = 1.0
    for dim, blocks in pieces:
        draws = jax.random.uniform(jax.random.fold_in(jax.random.fold_in(rng, 6), dim), (blocks,), jnp.float32, least / len(pieces), high / len(pieces))
        level = level * jnp.repeat(jnp.exp(draws), shape[dim] // blocks).reshape((-1,) + (1,) * (len(shape) - 1 - dim))
    return level


def deal_out(rng, own, number, rows, number_of, top, most, skew):
    order = jax.random.permutation(rng, number_of)
    heavy_load, common = load_shares(number_of, rows * top, most, skew, True), load_shares(number_of, rows * top, most, skew, False)
    places = jnp.arange(number_of)

    def named(sizes, turn):
        used = int((sizes > 0).sum())
        fixed = max(1, used // 4)
        shifted = fixed + (places - fixed + turn * (used - fixed)) % max(1, number_of - fixed)
        return jnp.zeros((number_of,), jnp.int32).at[order[jnp.where(places < fixed, places, shifted)]].set(jnp.asarray(sizes, jnp.int32))

    sizes = jnp.where(number % 4 == 0, named(heavy_load, number // 4), named(common, number - number // 4 - 1))
    mixed = jax.random.permutation(jax.random.fold_in(own, 3), number_of)
    donor, taker = mixed[0:number_of // 2 * 2:2], mixed[1:number_of // 2 * 2:2]
    margin = jnp.minimum(sizes[donor] - 1, most - sizes[taker]) // 2
    margin = jnp.where((donor == order[0]) | (taker == order[0]) | (sizes[taker] == 0), 0, jnp.maximum(margin, 0))
    shifted = jax.random.randint(jax.random.fold_in(own, 4), (number_of // 2,), 0, 1 << 20) % (margin + 1)
    sizes = sizes.at[donor].add(-shifted).at[taker].add(shifted)
    labels = jnp.searchsorted(jnp.cumsum(sizes), jnp.arange(rows * top), side="right").astype(jnp.int32)
    table = labels.reshape(top, rows).T
    table = table[jax.random.permutation(jax.random.fold_in(own, 1), rows)]
    turn = jax.random.randint(jax.random.fold_in(own, 2), (rows, 1), 0, top)
    return jnp.take_along_axis(table, (jnp.arange(top)[None, :] + turn) % top, axis=1)


def load_shares(count, total, reach, lean, full):
    weights = [(1 << 20) // math.isqrt(standing ** lean) + 1 for standing in range(1, count + 1)]
    largest = reach if full else min(reach, max(-(-total // count), total * weights[0] // sum(weights)))
    least = 1 if total - largest >= count - 1 else 0
    given, rest = [largest] + [least] * (count - 1), total - largest - least * (count - 1)
    while rest > 0:
        movable = [i for i in range(1, count) if given[i] < largest] or [i for i in range(1, count) if given[i] < reach]
        pool, budget = sum([weights[i] for i in movable]), rest
        for i in movable:
            extra = min(reach - given[i], max(1, budget * weights[i] // pool), rest)
            given[i] = given[i] + extra
            rest = rest - extra
    return np.array(given)


def noise(key, shape, deviation, bound, pieces=(), held_as=jnp.bfloat16):
    array = deviation * jax.random.normal(key, shape, jnp.float32)
    if pieces:
        array = array * shard_levels(key, shape, pieces, -0.22, 0.18)
    return jnp.clip(array, -bound, bound).astype(held_as)


def setup_inputs(seed: int = 0, part: int = 0) -> dict:
    keys = jax.random.split(jax.random.key(seed), 14)
    part_splits = jax.random.split(jax.random.fold_in(keys[13], part), 14)
    queries = draw_queries(jax.random.fold_in(jax.random.fold_in(keys[13], part), 71), part)
    key_cache = draw_key_cache(jax.random.fold_in(jax.random.fold_in(keys[13], part), 71), part)
    value_cache = noise(part_splits[2], (TOTAL, KVH, L, HD), 1.0, 6.0, ((0, 16),))
    new_key = noise(part_splits[3], (TOTAL, KVH * HD), 1.0, 6.0, ((0, 16),))
    new_value = noise(part_splits[4], (TOTAL, KVH * HD), 1.0, 6.0, ((0, 16),))
    lengths = draw_lengths(jax.random.fold_in(jax.random.fold_in(keys[13], part), 71), part)
    residual = draw_residual(jax.random.fold_in(jax.random.fold_in(keys[13], part), 71), part)
    norm_gain = jnp.clip(1.0 + 0.18 * jax.random.normal(keys[7], (D,), jnp.float32), 0.099609375, 1.8984375).astype(jnp.bfloat16)
    expert_ids_keys = jax.random.split(jax.random.fold_in(part_splits[8], 1), TOTAL // ROWS)
    expert_ids_turns = jax.random.permutation(jax.random.fold_in(part_splits[8], 3), TOTAL // ROWS)
    expert_ids = jax.vmap(lambda own, number: deal_out(jax.random.fold_in(part_splits[8], 2), own, number, ROWS, EXPERTS, TOPK, CAP, 2))(expert_ids_keys, expert_ids_turns).reshape((TOTAL, TOPK))
    gate_probs = jnp.clip(jnp.exp(math.log(1.0) - 2.3025851 * jax.random.uniform(part_splits[9], (TOTAL, TOPK), jnp.float32) ** shard_levels(part_splits[9], (TOTAL, TOPK), ((0, 16),), -0.2, 0.2)), 0.1, 1.0)
    gate_proj = noise(keys[10], (EXPERTS, D, FFE), D ** -0.5, 0.09375, ((0, 16),))
    up_proj = noise(keys[11], (EXPERTS, D, FFE), D ** -0.5, 0.09375, ((0, 16),))
    down_proj = noise(keys[12], (EXPERTS, FFE, D), FFE ** -0.5, 0.21875, ((0, 16),))
    return {"queries": queries, "key_cache": key_cache, "value_cache": value_cache, "new_key": new_key, "new_value": new_value, "lengths": lengths, "residual": residual, "norm_gain": norm_gain, "expert_ids": expert_ids, "gate_probs": gate_probs, "gate_proj": gate_proj, "up_proj": up_proj, "down_proj": down_proj}


def attend(queries, key_cache, value_cache, new_key, new_value, lengths):
    row_count = queries.shape[0]
    groups_kv = key_cache.shape[1]
    head_dim = key_cache.shape[3]
    per_group = queries.shape[1] // (groups_kv * head_dim)
    scaling = 1.0 / math.sqrt(head_dim)
    query_blocks = queries.reshape(row_count, groups_kv, per_group, head_dim).astype(jnp.float32)
    cached = jnp.einsum('rghd,rgpd->rghp', query_blocks, key_cache.astype(jnp.float32)) * scaling
    fresh_keys = new_key.reshape(row_count, groups_kv, head_dim).astype(jnp.float32)
    own_score = jnp.einsum('rghd,rgd->rgh', query_blocks, fresh_keys) * scaling
    position = lax.broadcasted_iota(jnp.int32, cached.shape, 3)
    valid_keys = position < lengths.astype(jnp.int32)[:, None, None, None]
    cached = jnp.where(valid_keys, cached, -jnp.inf)
    largest = jnp.maximum(lax.optimization_barrier(jnp.max(cached, axis=3)), own_score)
    exp_cached = jnp.exp(cached - largest[..., None])
    own_exp = jnp.exp(own_score - largest)
    denominator = lax.optimization_barrier(jnp.sum(exp_cached, axis=3)) + own_exp
    weights = (exp_cached / denominator[..., None]).astype(jnp.bfloat16)
    own_weight = (own_exp / denominator).astype(jnp.bfloat16)
    fresh_values = new_value.reshape(row_count, groups_kv, head_dim).astype(jnp.float32)
    attended = jnp.einsum('rghp,rgpd->rghd', weights.astype(jnp.float32), value_cache.astype(jnp.float32))
    attended = attended + own_weight.astype(jnp.float32)[..., None] * fresh_values[:, :, None, :]
    return attended.reshape(row_count, per_group * groups_kv * head_dim)

def slot_codes(expert_ids, block_rows):
    total_rows, top_count = expert_ids.shape
    blocks = expert_ids.reshape(total_rows // block_rows, block_rows * top_count)
    matches = blocks[:, :, None] == blocks[:, None, :]
    earlier = lax.broadcasted_iota(jnp.int32, matches.shape, 2) < lax.broadcasted_iota(jnp.int32, matches.shape, 1)
    slot_index = lax.optimization_barrier(jnp.sum((matches & earlier).astype(jnp.int32), axis=2))
    return slot_index.reshape(total_rows, top_count)

def reference(queries, key_cache, value_cache, new_key, new_value, lengths, residual, norm_gain, expert_ids, gate_probs, gate_proj, up_proj, down_proj):
    attended = attend(queries, key_cache, value_cache, new_key, new_value, lengths)
    hidden = (residual.astype(jnp.float32) + attended).astype(jnp.bfloat16)
    widened = hidden.astype(jnp.float32)
    meansq = lax.optimization_barrier(jnp.mean(widened * widened, axis=1, keepdims=True))
    normed = (widened * lax.rsqrt(meansq + 1e-06) * norm_gain.astype(jnp.float32)[None, :]).astype(jnp.bfloat16)
    slot_index = slot_codes(expert_ids, ROWS)
    total_rows = ROWS * N_ATT
    row_index = lax.broadcasted_iota(jnp.int32, expert_ids.shape, 0)
    owner_block = row_index // ROWS
    slot_table = jnp.full((EXPERTS, N_ATT, CAP), total_rows, jnp.int32)
    slot_table = slot_table.at[expert_ids, owner_block, slot_index].set(row_index)
    padded = jnp.concatenate([normed, jnp.zeros((1, D), jnp.bfloat16)], axis=0)

    def expert_apply(expert_index):
        picked = padded[slot_table[expert_index].reshape(-1)]
        gate_act = jnp.dot(picked, gate_proj[expert_index], preferred_element_type=jnp.float32)
        up_act = jnp.dot(picked, up_proj[expert_index], preferred_element_type=jnp.float32)
        inner_act = (jax.nn.silu(gate_act) * up_act).astype(jnp.bfloat16)
        return jnp.dot(inner_act, down_proj[expert_index], preferred_element_type=jnp.float32).astype(jnp.bfloat16)
    outputs = lax.map(expert_apply, jnp.arange(EXPERTS, dtype=jnp.int32))
    flat_out = outputs.reshape(EXPERTS * N_ATT * CAP, D)
    lookup = ((expert_ids * N_ATT + owner_block) * CAP + slot_index).astype(jnp.int32)
    chosen = flat_out[lookup].astype(jnp.float32)
    share_norm = gate_probs / lax.optimization_barrier(jnp.sum(gate_probs, axis=1, keepdims=True))
    combined = lax.optimization_barrier(jnp.sum(share_norm[:, :, None] * chosen, axis=1))
    return (widened + combined).astype(jnp.bfloat16)
```

```python
import math

import jax
import jax.numpy as jnp
from jax import lax
from jax.sharding import PartitionSpec as P


def attend(queries, key_cache, value_cache, new_key, new_value, lengths):
    row_count = queries.shape[0]
    groups_kv = key_cache.shape[1]
    head_dim = key_cache.shape[3]
    per_group = queries.shape[1] // (groups_kv * head_dim)
    scaling = 1.0 / math.sqrt(head_dim)
    query_blocks = queries.reshape(row_count, groups_kv, per_group, head_dim)
    cached = (
        jnp.einsum("rghd,rgpd->rghp", query_blocks, key_cache, preferred_element_type=jnp.float32)
        * scaling
    )
    fresh_keys = new_key.reshape(row_count, groups_kv, head_dim)
    own_score = (
        jnp.einsum("rghd,rgd->rgh", query_blocks, fresh_keys, preferred_element_type=jnp.float32)
        * scaling
    )
    position = lax.broadcasted_iota(jnp.int32, cached.shape, 3)
    valid_keys = position < lengths[:, None, None, None]
    cached = jnp.where(valid_keys, cached, -jnp.inf)
    largest = jnp.maximum(jnp.max(cached, axis=3), own_score)
    exp_cached = jnp.exp(cached - largest[..., None])
    own_exp = jnp.exp(own_score - largest)
    denominator = jnp.sum(exp_cached, axis=3) + own_exp
    weights = (exp_cached / denominator[..., None]).astype(jnp.bfloat16)
    own_weight = (own_exp / denominator).astype(jnp.bfloat16)
    fresh_values = new_value.reshape(row_count, groups_kv, head_dim).astype(jnp.float32)
    attended = jnp.einsum(
        "rghp,rgpd->rghd", weights, value_cache, preferred_element_type=jnp.float32
    )
    attended = attended + own_weight.astype(jnp.float32)[..., None] * fresh_values[:, :, None, :]
    return attended.reshape(row_count, per_group * groups_kv * head_dim)


def body(
    queries,
    key_cache,
    value_cache,
    new_key,
    new_value,
    lengths,
    residual,
    norm_gain,
    expert_ids,
    gate_probs,
    gate_proj,
    up_proj,
    down_proj,
):
    attended = attend(queries, key_cache, value_cache, new_key, new_value, lengths)
    hidden = (residual.astype(jnp.float32) + attended).astype(jnp.bfloat16)
    local_rows, top_count = expert_ids.shape
    width_full = down_proj.shape[2]
    owners = lax.axis_size("att")
    local_experts = gate_proj.shape[0]
    experts_all = owners * local_experts
    capacity = min(local_rows, max(2, 2 * local_rows * top_count // experts_all))
    full_rows, full_gain = (
        lax.all_gather(hidden, "exp", axis=1, tiled=True),
        lax.all_gather(norm_gain, "exp", axis=0, tiled=True),
    )
    widened = full_rows.astype(jnp.float32)
    meansq = jnp.sum(widened * widened, axis=1, keepdims=True) / width_full
    normed = (widened * lax.rsqrt(meansq + 1e-06) * full_gain.astype(jnp.float32)[None, :]).astype(
        jnp.bfloat16
    )
    flat_ids = expert_ids.reshape(-1)
    matches = flat_ids[:, None] == flat_ids[None, :]
    earlier = lax.broadcasted_iota(jnp.int32, matches.shape, 1) < lax.broadcasted_iota(
        jnp.int32, matches.shape, 0
    )
    slot_index = jnp.sum((matches & earlier).astype(jnp.int32), axis=1).reshape(
        local_rows, top_count
    )
    target_codes = expert_ids * capacity + slot_index
    targets = lax.broadcasted_iota(jnp.int32, (experts_all * capacity, local_rows, top_count), 0)
    placed = (targets == target_codes[None, :, :]).astype(jnp.float32)
    dispatch = jnp.sum(placed, axis=2).astype(jnp.bfloat16)
    outgoing = jnp.dot(dispatch, normed, preferred_element_type=jnp.float32).astype(jnp.bfloat16)
    outgoing = outgoing.reshape(experts_all, capacity, normed.shape[1])
    arrived = lax.all_to_all(outgoing, "att", split_axis=0, concat_axis=0, tiled=True)
    arrived = arrived.reshape(owners, local_experts, capacity, width_full)
    gate_act = jnp.einsum("secd,edf->secf", arrived, gate_proj, preferred_element_type=jnp.float32)
    up_act = jnp.einsum("secd,edf->secf", arrived, up_proj, preferred_element_type=jnp.float32)
    inner_act = (jax.nn.silu(gate_act) * up_act).astype(jnp.bfloat16)
    partial_out = jnp.einsum(
        "secf,efd->secd", inner_act, down_proj, preferred_element_type=jnp.float32
    )
    returned = lax.psum_scatter(
        partial_out.astype(jnp.bfloat16), "exp", scatter_dimension=3, tiled=True
    )
    returned_rows = lax.all_to_all(returned, "att", split_axis=0, concat_axis=0, tiled=True)
    returned_rows = returned_rows.reshape(experts_all * capacity, returned_rows.shape[3]).astype(
        jnp.float32
    )
    share_norm = gate_probs / jnp.sum(gate_probs, axis=1, keepdims=True)
    combine_table = jnp.sum(placed * share_norm[None, :, :], axis=2)
    combined = jnp.dot(combine_table.T, returned_rows, precision=lax.Precision.HIGHEST)
    return (hidden.astype(jnp.float32) + combined).astype(jnp.bfloat16)


def norm_rows(hidden, norm_gain):
    widened = hidden.astype(jnp.float32)
    meansq = jnp.sum(widened * widened, axis=1, keepdims=True) / hidden.shape[1]
    return (widened * lax.rsqrt(meansq + 1e-06) * norm_gain.astype(jnp.float32)[None, :]).astype(
        jnp.bfloat16
    )


def share_table(expert_ids, gate_probs, experts_all):
    share_norm = gate_probs / jnp.sum(gate_probs, axis=1, keepdims=True)
    hits = expert_ids[:, :, None] == jnp.arange(experts_all, dtype=jnp.int32)[None, None, :]
    return jnp.sum(jnp.where(hits, share_norm[:, :, None], 0.0), axis=1)


def dense_body(
    queries,
    key_cache,
    value_cache,
    new_key,
    new_value,
    lengths,
    residual,
    norm_gain,
    expert_ids,
    gate_probs,
    gate_proj,
    up_proj,
    down_proj,
):
    attended = attend(queries, key_cache, value_cache, new_key, new_value, lengths)
    hidden = (residual.astype(jnp.float32) + attended).astype(jnp.bfloat16)
    normed = norm_rows(hidden, norm_gain)
    owners = lax.axis_size("att")
    me = lax.axis_index("att")
    shares = share_table(expert_ids, gate_probs, owners)
    all_shares = lax.all_gather(shares, "att", axis=0, tiled=True)
    own_share = lax.dynamic_slice_in_dim(all_shares, me, 1, axis=1)
    rows = lax.all_gather(normed, "att", axis=0, tiled=True)
    gate_act = jnp.dot(rows, gate_proj[0], preferred_element_type=jnp.float32)
    up_act = jnp.dot(rows, up_proj[0], preferred_element_type=jnp.float32)
    inner_act = (jax.nn.silu(gate_act) * up_act).astype(jnp.bfloat16)
    out = jnp.dot(inner_act, down_proj[0], preferred_element_type=jnp.float32)
    weighted = (out.astype(jnp.bfloat16).astype(jnp.float32) * own_share).astype(jnp.bfloat16)
    combined = lax.psum_scatter(weighted, "att", scatter_dimension=0, tiled=True)
    return (hidden.astype(jnp.float32) + combined.astype(jnp.float32)).astype(jnp.bfloat16)


def pick_body(*args):
    local_rows, top_count = args[8].shape
    experts_all = lax.axis_size("att") * args[10].shape[0]
    capacity = min(local_rows, max(2, 2 * local_rows * top_count // experts_all))
    if lax.axis_size("exp") == 1 and args[10].shape[0] == 1 and capacity == local_rows:
        return dense_body(*args)
    return body(*args)


def solution(mesh):
    return jax.shard_map(
        pick_body,
        mesh=mesh,
        in_specs=(
            P(("groups", "att"), "exp"),
            P(("groups", "att"), "exp", None, None),
            P(("groups", "att"), "exp", None, None),
            P(("groups", "att"), "exp"),
            P(("groups", "att"), "exp"),
            P(("groups", "att")),
            P(("groups", "att"), "exp"),
            P("exp"),
            P(("groups", "att"), None),
            P(("groups", "att"), None),
            P("att", None, "exp"),
            P("att", None, "exp"),
            P("att", "exp", None),
        ),
        out_specs=P(("groups", "att"), "exp"),
        check_vma=False,
    )
```

```python
import math

import jax
import jax.numpy as jnp
from jax import lax
from jax.experimental import pallas as pl
from jax.experimental.pallas import tpu as pltpu
from jax.sharding import PartitionSpec as P


def attend(queries, key_cache, value_cache, new_key, new_value, lengths):
    row_count = queries.shape[0]
    groups_kv = key_cache.shape[1]
    head_dim = key_cache.shape[3]
    per_group = queries.shape[1] // (groups_kv * head_dim)
    scaling = 1.0 / math.sqrt(head_dim)
    query_blocks = queries.reshape(row_count, groups_kv, per_group, head_dim)
    cached = (
        jnp.einsum("rghd,rgpd->rghp", query_blocks, key_cache, preferred_element_type=jnp.float32)
        * scaling
    )
    fresh_keys = new_key.reshape(row_count, groups_kv, head_dim)
    own_score = (
        jnp.einsum("rghd,rgd->rgh", query_blocks, fresh_keys, preferred_element_type=jnp.float32)
        * scaling
    )
    position = lax.broadcasted_iota(jnp.int32, cached.shape, 3)
    valid_keys = position < lengths[:, None, None, None]
    cached = jnp.where(valid_keys, cached, -jnp.inf)
    largest = jnp.maximum(jnp.max(cached, axis=3), own_score)
    exp_cached = jnp.exp(cached - largest[..., None])
    own_exp = jnp.exp(own_score - largest)
    denominator = jnp.sum(exp_cached, axis=3) + own_exp
    weights = (exp_cached / denominator[..., None]).astype(jnp.bfloat16)
    own_weight = (own_exp / denominator).astype(jnp.bfloat16)
    fresh_values = new_value.reshape(row_count, groups_kv, head_dim).astype(jnp.float32)
    attended = jnp.einsum(
        "rghp,rgpd->rghd", weights, value_cache, preferred_element_type=jnp.float32
    )
    attended = attended + own_weight.astype(jnp.float32)[..., None] * fresh_values[:, :, None, :]
    return attended.reshape(row_count, per_group * groups_kv * head_dim)


def body(
    queries,
    key_cache,
    value_cache,
    new_key,
    new_value,
    lengths,
    residual,
    norm_gain,
    expert_ids,
    gate_probs,
    gate_proj,
    up_proj,
    down_proj,
):
    attended = attend(queries, key_cache, value_cache, new_key, new_value, lengths)
    hidden = (residual.astype(jnp.float32) + attended).astype(jnp.bfloat16)
    local_rows, top_count = expert_ids.shape
    width_full = down_proj.shape[2]
    owners = lax.axis_size("att")
    local_experts = gate_proj.shape[0]
    experts_all = owners * local_experts
    capacity = min(local_rows, max(2, 2 * local_rows * top_count // experts_all))
    full_rows, full_gain = (
        lax.all_gather(hidden, "exp", axis=1, tiled=True),
        lax.all_gather(norm_gain, "exp", axis=0, tiled=True),
    )
    widened = full_rows.astype(jnp.float32)
    meansq = jnp.sum(widened * widened, axis=1, keepdims=True) / width_full
    normed = (widened * lax.rsqrt(meansq + 1e-06) * full_gain.astype(jnp.float32)[None, :]).astype(
        jnp.bfloat16
    )
    flat_ids = expert_ids.reshape(-1)
    matches = flat_ids[:, None] == flat_ids[None, :]
    earlier = lax.broadcasted_iota(jnp.int32, matches.shape, 1) < lax.broadcasted_iota(
        jnp.int32, matches.shape, 0
    )
    slot_index = jnp.sum((matches & earlier).astype(jnp.int32), axis=1).reshape(
        local_rows, top_count
    )
    target_codes = expert_ids * capacity + slot_index
    targets = lax.broadcasted_iota(jnp.int32, (experts_all * capacity, local_rows, top_count), 0)
    placed = (targets == target_codes[None, :, :]).astype(jnp.float32)
    dispatch = jnp.sum(placed, axis=2).astype(jnp.bfloat16)
    outgoing = jnp.dot(dispatch, normed, preferred_element_type=jnp.float32).astype(jnp.bfloat16)
    outgoing = outgoing.reshape(experts_all, capacity, normed.shape[1])
    arrived = lax.all_to_all(outgoing, "att", split_axis=0, concat_axis=0, tiled=True)
    arrived = arrived.reshape(owners, local_experts, capacity, width_full)
    gate_act = jnp.einsum("secd,edf->secf", arrived, gate_proj, preferred_element_type=jnp.float32)
    up_act = jnp.einsum("secd,edf->secf", arrived, up_proj, preferred_element_type=jnp.float32)
    inner_act = (jax.nn.silu(gate_act) * up_act).astype(jnp.bfloat16)
    partial_out = jnp.einsum(
        "secf,efd->secd", inner_act, down_proj, preferred_element_type=jnp.float32
    )
    returned = lax.psum_scatter(
        partial_out.astype(jnp.bfloat16), "exp", scatter_dimension=3, tiled=True
    )
    returned_rows = lax.all_to_all(returned, "att", split_axis=0, concat_axis=0, tiled=True)
    returned_rows = returned_rows.reshape(experts_all * capacity, returned_rows.shape[3]).astype(
        jnp.float32
    )
    share_norm = gate_probs / jnp.sum(gate_probs, axis=1, keepdims=True)
    combine_table = jnp.sum(placed * share_norm[None, :, :], axis=2)
    combined = jnp.dot(combine_table.T, returned_rows, precision=lax.Precision.HIGHEST)
    return (hidden.astype(jnp.float32) + combined).astype(jnp.bfloat16)


def norm_rows(hidden, norm_gain):
    widened = hidden.astype(jnp.float32)
    meansq = jnp.sum(widened * widened, axis=1, keepdims=True) / hidden.shape[1]
    return (widened * lax.rsqrt(meansq + 1e-06) * norm_gain.astype(jnp.float32)[None, :]).astype(
        jnp.bfloat16
    )


def share_table(expert_ids, gate_probs, experts_all):
    share_norm = gate_probs / jnp.sum(gate_probs, axis=1, keepdims=True)
    hits = expert_ids[:, :, None] == jnp.arange(experts_all, dtype=jnp.int32)[None, None, :]
    return jnp.sum(jnp.where(hits, share_norm[:, :, None], 0.0), axis=1)


def expert_kernel(
    block_ref,
    hidden_ref,
    gate_hbm,
    up_hbm,
    down_hbm,
    out_ref,
    rows,
    part,
    got,
    inner,
    gate,
    up,
    down,
    weight_sem,
    row_send,
    row_recv,
    sum_send,
    sum_recv,
):
    me = lax.axis_index("att")
    partners = {m: me + m - 2 * m * (lax.div(me, m) % 2) for m in (1, 2, 4, 8)}
    block_rows, width = hidden_ref.shape

    barrier = pltpu.get_barrier_semaphore()
    for m in (1, 2, 4, 8):
        pl.semaphore_signal(
            barrier, inc=1, device_id={"att": partners[m]}, device_id_type=pl.DeviceIdType.MESH
        )
    loads = [
        pltpu.make_async_copy(source, held, weight_sem.at[i])
        for i, (source, held) in enumerate(((gate_hbm, gate), (up_hbm, up), (down_hbm, down)))
    ]
    for load in loads:
        load.start()
    pl.semaphore_wait(barrier, 4)

    sent = {}

    def forward(slot, *masks):
        for m in masks:
            copy = pltpu.make_async_remote_copy(
                src_ref=block_ref if slot == 0 else rows.at[slot],
                dst_ref=rows.at[slot + m],
                send_sem=row_send.at[slot + m],
                recv_sem=row_recv.at[slot + m],
                device_id={"att": partners[m]},
                device_id_type=pl.DeviceIdType.MESH,
            )
            copy.start()
            sent["row", slot + m] = copy

    def arrived(*slots):
        for slot in slots:
            sent["row", slot].wait_recv()

    def send_sum(slot, m, place):
        copy = pltpu.make_async_remote_copy(
            src_ref=part.at[slot],
            dst_ref=got.at[place],
            send_sem=sum_send.at[place],
            recv_sem=sum_recv.at[place],
            device_id={"att": partners[m]},
            device_id_type=pl.DeviceIdType.MESH,
        )
        copy.start()
        sent["sum", place] = copy

    def add(slot, place):
        sent["sum", place].wait_recv()
        part[slot] = (part[slot].astype(jnp.float32) + got[place].astype(jnp.float32)).astype(
            jnp.bfloat16
        )

    def experts(chunk):
        first, count = 4 * chunk, 4
        length = count * block_rows

        def hidden_step(j, carry):
            columns = pl.ds(pl.multiple_of(j * 256, 256), 256)
            held = rows[first : first + count, :, :width].reshape(length, width)
            g = jnp.dot(held, gate[:, columns], preferred_element_type=jnp.float32)
            u = jnp.dot(held, up[:, columns], preferred_element_type=jnp.float32)
            inner[:, columns] = (g / (1.0 + jnp.exp(-g)) * u).astype(jnp.bfloat16)
            return carry

        lax.fori_loop(0, gate.shape[1] // 256, hidden_step, 0)
        pieces = rows[first : first + count, :, width:].reshape(length, 128).astype(jnp.float32)
        lane = lax.broadcasted_iota(jnp.int32, pieces.shape, 1)
        mine = (lane == me) | (lane == me + 16) | (lane == me + 32)
        share = jnp.sum(jnp.where(mine, pieces, 0.0), axis=1, keepdims=True)

        def out_step(j, carry):
            columns = pl.ds(pl.multiple_of(j * 512, 512), 512)
            o = jnp.dot(inner[...], down[:, columns], preferred_element_type=jnp.float32)
            o = (o.astype(jnp.bfloat16).astype(jnp.float32) * share).astype(jnp.bfloat16)
            part[first : first + count, :, columns] = o.reshape(count, block_rows, 512)
            return carry

        lax.fori_loop(0, width // 512, out_step, 0)
        for xr in (0, 1):
            send_sum(first + 2 * xr + 1, 1, 2 * chunk + xr)

    def across_x(chunk):
        add(4 * chunk + 2, 2 * chunk + 1)
        send_sum(4 * chunk + 2, 2, 8 + chunk)
        add(4 * chunk, 2 * chunk)

    forward(0, 2, 4, 8, 1)
    rows[0] = block_ref[...]
    arrived(4)
    forward(4, 2, 8, 1)
    arrived(2)
    forward(2, 1)
    arrived(8)
    forward(8, 2, 1)
    for load in loads:
        load.wait()
    arrived(1, 3)
    experts(0)
    arrived(6)
    forward(6, 1)
    arrived(12)
    forward(12, 2, 1)
    across_x(0)
    arrived(5, 7)
    experts(1)
    arrived(10)
    forward(10, 1)
    across_x(1)
    arrived(9, 11)
    experts(2)
    arrived(14)
    forward(14, 1)
    across_x(2)
    arrived(13, 15)
    experts(3)
    across_x(3)
    add(8, 10)
    send_sum(8, 8, 12)
    add(12, 11)
    send_sum(12, 8, 13)
    add(0, 8)
    add(4, 9)
    add(4, 13)
    send_sum(4, 4, 14)
    add(0, 12)
    sent["sum", 14].wait_recv()
    total = part[0].astype(jnp.float32) + got[14].astype(jnp.float32)
    out_ref[...] = (hidden_ref[...].astype(jnp.float32) + total).astype(jnp.bfloat16)
    for copy in sent.values():
        copy.wait_send()


def dense_body(
    queries,
    key_cache,
    value_cache,
    new_key,
    new_value,
    lengths,
    residual,
    norm_gain,
    expert_ids,
    gate_probs,
    gate_proj,
    up_proj,
    down_proj,
):
    attended = attend(queries, key_cache, value_cache, new_key, new_value, lengths)
    hidden = (residual.astype(jnp.float32) + attended).astype(jnp.bfloat16)
    normed = norm_rows(hidden, norm_gain)
    owners = lax.axis_size("att")
    local_rows, width = hidden.shape
    units = gate_proj.shape[2]
    rest, terms = share_table(expert_ids, gate_probs, owners), []
    for _ in range(3):
        term = lax.reduce_precision(rest, 8, 7)
        terms.append(term.astype(jnp.bfloat16))
        rest = rest - term
    spare = jnp.zeros((local_rows, 128 - 3 * owners), jnp.bfloat16)
    block = jnp.concatenate([normed, *terms, spare], axis=1)
    weight = gate_proj.size + up_proj.size + down_proj.size
    vmem = pl.BlockSpec(memory_space=pltpu.VMEM)
    hbm = pl.BlockSpec(memory_space=pl.ANY)
    return pl.pallas_call(
        expert_kernel,
        out_shape=jax.ShapeDtypeStruct((local_rows, width), jnp.bfloat16),
        in_specs=[vmem, vmem, hbm, hbm, hbm],
        out_specs=vmem,
        scratch_shapes=[
            pltpu.VMEM((owners, local_rows, block.shape[1]), jnp.bfloat16),
            pltpu.VMEM((owners, local_rows, width), jnp.bfloat16),
            pltpu.VMEM((owners, local_rows, width), jnp.bfloat16),
            pltpu.VMEM((4 * local_rows, units), jnp.bfloat16),
            pltpu.VMEM((width, units), jnp.bfloat16),
            pltpu.VMEM((width, units), jnp.bfloat16),
            pltpu.VMEM((units, width), jnp.bfloat16),
            pltpu.SemaphoreType.DMA((3,)),
            pltpu.SemaphoreType.DMA((16,)),
            pltpu.SemaphoreType.DMA((16,)),
            pltpu.SemaphoreType.DMA((16,)),
            pltpu.SemaphoreType.DMA((16,)),
        ],
        compiler_params=pltpu.CompilerParams(
            collective_id=0, has_side_effects=True, vmem_limit_bytes=48 * 1024 * 1024
        ),
        cost_estimate=pl.CostEstimate(
            flops=2 * owners * local_rows * weight,
            bytes_accessed=2 * weight,
            transcendentals=owners * local_rows * units,
        ),
    )(block, hidden, gate_proj[0], up_proj[0], down_proj[0])


def pick_body(*args):
    local_rows, top_count = args[8].shape
    experts_all = lax.axis_size("att") * args[10].shape[0]
    capacity = min(local_rows, max(2, 2 * local_rows * top_count // experts_all))
    dense = lax.axis_size("exp") == 1 and args[10].shape[0] == 1 and capacity == local_rows
    if dense and lax.axis_size("att") == 16:
        return dense_body(*args)
    return body(*args)


def solution(mesh):
    return jax.shard_map(
        pick_body,
        mesh=mesh,
        in_specs=(
            P(("groups", "att"), "exp"),
            P(("groups", "att"), "exp", None, None),
            P(("groups", "att"), "exp", None, None),
            P(("groups", "att"), "exp"),
            P(("groups", "att"), "exp"),
            P(("groups", "att")),
            P(("groups", "att"), "exp"),
            P("exp"),
            P(("groups", "att"), None),
            P(("groups", "att"), None),
            P("att", None, "exp"),
            P("att", None, "exp"),
            P("att", "exp", None),
        ),
        out_specs=P(("groups", "att"), "exp"),
        check_vma=False,
    )
```

```python
import functools
import math

import jax
import jax.numpy as jnp
from jax import lax
from jax.experimental import pallas as pl
from jax.experimental.pallas import tpu as pltpu
from jax.sharding import PartitionSpec as P


def attend(queries, key_cache, value_cache, new_key, new_value, lengths):
    row_count = queries.shape[0]
    groups_kv = key_cache.shape[1]
    head_dim = key_cache.shape[3]
    per_group = queries.shape[1] // (groups_kv * head_dim)
    scaling = 1.0 / math.sqrt(head_dim)
    query_blocks = queries.reshape(row_count, groups_kv, per_group, head_dim)
    cached = (
        jnp.einsum("rghd,rgpd->rghp", query_blocks, key_cache, preferred_element_type=jnp.float32)
        * scaling
    )
    fresh_keys = new_key.reshape(row_count, groups_kv, head_dim)
    own_score = (
        jnp.einsum("rghd,rgd->rgh", query_blocks, fresh_keys, preferred_element_type=jnp.float32)
        * scaling
    )
    position = lax.broadcasted_iota(jnp.int32, cached.shape, 3)
    valid_keys = position < lengths[:, None, None, None]
    cached = jnp.where(valid_keys, cached, -jnp.inf)
    largest = jnp.maximum(jnp.max(cached, axis=3), own_score)
    exp_cached = jnp.exp(cached - largest[..., None])
    own_exp = jnp.exp(own_score - largest)
    denominator = jnp.sum(exp_cached, axis=3) + own_exp
    weights = (exp_cached / denominator[..., None]).astype(jnp.bfloat16)
    own_weight = (own_exp / denominator).astype(jnp.bfloat16)
    fresh_values = new_value.reshape(row_count, groups_kv, head_dim).astype(jnp.float32)
    attended = jnp.einsum(
        "rghp,rgpd->rghd", weights, value_cache, preferred_element_type=jnp.float32
    )
    attended = attended + own_weight.astype(jnp.float32)[..., None] * fresh_values[:, :, None, :]
    return attended.reshape(row_count, per_group * groups_kv * head_dim)


def body(
    queries,
    key_cache,
    value_cache,
    new_key,
    new_value,
    lengths,
    residual,
    norm_gain,
    expert_ids,
    gate_probs,
    gate_proj,
    up_proj,
    down_proj,
):
    attended = attend(queries, key_cache, value_cache, new_key, new_value, lengths)
    hidden = (residual.astype(jnp.float32) + attended).astype(jnp.bfloat16)
    local_rows, top_count = expert_ids.shape
    width_full = down_proj.shape[2]
    owners = lax.axis_size("att")
    local_experts = gate_proj.shape[0]
    experts_all = owners * local_experts
    capacity = min(local_rows, max(2, 2 * local_rows * top_count // experts_all))
    full_rows, full_gain = (
        lax.all_gather(hidden, "exp", axis=1, tiled=True),
        lax.all_gather(norm_gain, "exp", axis=0, tiled=True),
    )
    widened = full_rows.astype(jnp.float32)
    meansq = jnp.sum(widened * widened, axis=1, keepdims=True) / width_full
    normed = (widened * lax.rsqrt(meansq + 1e-06) * full_gain.astype(jnp.float32)[None, :]).astype(
        jnp.bfloat16
    )
    flat_ids = expert_ids.reshape(-1)
    matches = flat_ids[:, None] == flat_ids[None, :]
    earlier = lax.broadcasted_iota(jnp.int32, matches.shape, 1) < lax.broadcasted_iota(
        jnp.int32, matches.shape, 0
    )
    slot_index = jnp.sum((matches & earlier).astype(jnp.int32), axis=1).reshape(
        local_rows, top_count
    )
    target_codes = expert_ids * capacity + slot_index
    targets = lax.broadcasted_iota(jnp.int32, (experts_all * capacity, local_rows, top_count), 0)
    placed = (targets == target_codes[None, :, :]).astype(jnp.float32)
    dispatch = jnp.sum(placed, axis=2).astype(jnp.bfloat16)
    outgoing = jnp.dot(dispatch, normed, preferred_element_type=jnp.float32).astype(jnp.bfloat16)
    outgoing = outgoing.reshape(experts_all, capacity, normed.shape[1])
    arrived = lax.all_to_all(outgoing, "att", split_axis=0, concat_axis=0, tiled=True)
    arrived = arrived.reshape(owners, local_experts, capacity, width_full)
    gate_act = jnp.einsum("secd,edf->secf", arrived, gate_proj, preferred_element_type=jnp.float32)
    up_act = jnp.einsum("secd,edf->secf", arrived, up_proj, preferred_element_type=jnp.float32)
    inner_act = (jax.nn.silu(gate_act) * up_act).astype(jnp.bfloat16)
    partial_out = jnp.einsum(
        "secf,efd->secd", inner_act, down_proj, preferred_element_type=jnp.float32
    )
    returned = lax.psum_scatter(
        partial_out.astype(jnp.bfloat16), "exp", scatter_dimension=3, tiled=True
    )
    returned_rows = lax.all_to_all(returned, "att", split_axis=0, concat_axis=0, tiled=True)
    returned_rows = returned_rows.reshape(experts_all * capacity, returned_rows.shape[3]).astype(
        jnp.float32
    )
    share_norm = gate_probs / jnp.sum(gate_probs, axis=1, keepdims=True)
    combine_table = jnp.sum(placed * share_norm[None, :, :], axis=2)
    combined = jnp.dot(combine_table.T, returned_rows, precision=lax.Precision.HIGHEST)
    return (hidden.astype(jnp.float32) + combined).astype(jnp.bfloat16)


def norm_rows(hidden, norm_gain):
    widened = hidden.astype(jnp.float32)
    meansq = jnp.sum(widened * widened, axis=1, keepdims=True) / hidden.shape[1]
    return (widened * lax.rsqrt(meansq + 1e-06) * norm_gain.astype(jnp.float32)[None, :]).astype(
        jnp.bfloat16
    )


def share_table(expert_ids, gate_probs, experts_all):
    share_norm = gate_probs / jnp.sum(gate_probs, axis=1, keepdims=True)
    hits = expert_ids[:, :, None] == jnp.arange(experts_all, dtype=jnp.int32)[None, None, :]
    return jnp.sum(jnp.where(hits, share_norm[:, :, None], 0.0), axis=1)


def expert_kernel(
    block_ref,
    hidden_ref,
    gate_hbm,
    up_hbm,
    down_hbm,
    out_ref,
    rows,
    part,
    got,
    inner,
    gate,
    up,
    down,
    weight_sem,
    send_sem,
    row_recv,
    sum_recv,
):
    me = lax.axis_index("att")
    layer = lax.div(me, 4)
    inner_z = (layer == 1) | (layer == 2)
    partners = {m: me + m - 2 * m * (lax.div(me, m) % 2) for m in (1, 2, 4)}
    partners[12] = me + 4 * (3 - 2 * layer)
    block_rows, width = hidden_ref.shape

    barrier = pltpu.get_barrier_semaphore()
    for m in (1, 2, 4, 12):
        pl.semaphore_signal(
            barrier, inc=1, device_id={"att": partners[m]}, device_id_type=pl.DeviceIdType.MESH
        )
    loads = [
        pltpu.make_async_copy(source, held, weight_sem.at[i])
        for i, (source, held) in enumerate(((gate_hbm, gate), (up_hbm, up), (down_hbm, down)))
    ]
    for load in loads:
        load.start()
    pl.semaphore_wait(barrier, 4)

    sent = []

    def start(copy, when):
        sent.append((copy, when))
        if when is None:
            copy.start()
        else:
            pl.when(when)(copy.start)

    def forward(slot, *masks, when=None):
        for m in masks:
            copy = pltpu.make_async_remote_copy(
                src_ref=block_ref if slot == 0 else rows.at[slot],
                dst_ref=rows.at[slot ^ m],
                send_sem=send_sem.at[len(sent)],
                recv_sem=row_recv.at[slot ^ m],
                device_id={"att": partners[m]},
                device_id_type=pl.DeviceIdType.MESH,
            )
            start(copy, when)

    def arrived(*slots):
        for slot in slots:
            pltpu.make_async_remote_copy(
                src_ref=rows.at[slot],
                dst_ref=rows.at[slot],
                send_sem=row_recv.at[slot],
                recv_sem=row_recv.at[slot],
                device_id={"att": partners[1]},
                device_id_type=pl.DeviceIdType.MESH,
            ).wait_recv()

    def send_sum(slot, m, place, when=None):
        copy = pltpu.make_async_remote_copy(
            src_ref=part.at[slot],
            dst_ref=got.at[place],
            send_sem=send_sem.at[len(sent)],
            recv_sem=sum_recv.at[place],
            device_id={"att": partners[m]},
            device_id_type=pl.DeviceIdType.MESH,
        )
        start(copy, when)

    def sum_arrived(place):
        pltpu.make_async_remote_copy(
            src_ref=got.at[place],
            dst_ref=got.at[place],
            send_sem=sum_recv.at[place],
            recv_sem=sum_recv.at[place],
            device_id={"att": partners[1]},
            device_id_type=pl.DeviceIdType.MESH,
        ).wait_recv()

    def add(slot, place):
        sum_arrived(place)
        part[slot] = (part[slot].astype(jnp.float32) + got[place].astype(jnp.float32)).astype(
            jnp.bfloat16
        )

    def experts(chunk):
        first, count = 4 * chunk, 4
        length = count * block_rows

        def hidden_step(j, carry):
            columns = pl.ds(pl.multiple_of(j * 256, 256), 256)
            held = rows[first : first + count, :, :width].reshape(length, width)
            g = jnp.dot(held, gate[:, columns], preferred_element_type=jnp.float32)
            u = jnp.dot(held, up[:, columns], preferred_element_type=jnp.float32)
            inner[:, columns] = (g / (1.0 + jnp.exp(-g)) * u).astype(jnp.bfloat16)
            return carry

        lax.fori_loop(0, gate.shape[1] // 256, hidden_step, 0)
        pieces = rows[first : first + count, :, width:].reshape(length, 128).astype(jnp.float32)
        lane = lax.broadcasted_iota(jnp.int32, pieces.shape, 1)
        mine = (lane == me) | (lane == me + 16) | (lane == me + 32)
        share = jnp.sum(jnp.where(mine, pieces, 0.0), axis=1, keepdims=True)

        def out_step(j, carry):
            columns = pl.ds(pl.multiple_of(j * 512, 512), 512)
            o = jnp.dot(inner[...], down[:, columns], preferred_element_type=jnp.float32)
            o = (o.astype(jnp.bfloat16).astype(jnp.float32) * share).astype(jnp.bfloat16)
            part[first : first + count, :, columns] = o.reshape(count, block_rows, 512)
            return carry

        lax.fori_loop(0, width // 512, out_step, 0)
        for xr in (0, 1):
            send_sum(first + 2 * xr + 1, 1, 2 * chunk + xr)

    def across_x(chunk):
        add(4 * chunk + 2, 2 * chunk + 1)
        send_sum(4 * chunk + 2, 2, 8 + chunk)
        add(4 * chunk, 2 * chunk)

    outer_z = jnp.logical_not(inner_z)
    forward(0, 2, 4)
    forward(0, 12, when=inner_z)
    forward(0, 1)
    rows[0] = block_ref[...]
    arrived(4)
    forward(4, 2)
    forward(4, 12, when=inner_z)
    forward(4, 1)
    pl.when(inner_z)(functools.partial(arrived, 12))
    forward(12, 4, when=inner_z)
    arrived(2)
    forward(2, 1)
    for load in loads:
        load.wait()
    arrived(1, 3)
    experts(0)
    arrived(8)
    forward(8, 2)
    forward(8, 4, when=inner_z)
    forward(8, 1)
    arrived(6)
    forward(6, 1)
    arrived(5, 7)
    experts(1)
    pl.when(outer_z)(functools.partial(arrived, 12))
    forward(12, 2, 1)
    arrived(10)
    forward(10, 1)
    arrived(9, 11)
    experts(2)
    across_x(2)
    arrived(14)
    forward(14, 1)
    arrived(13, 15)
    experts(3)
    across_x(3)
    across_x(1)
    add(8, 10)
    send_sum(8, 4, 12, when=outer_z)
    add(12, 11)
    send_sum(12, 4, 13, when=outer_z)
    across_x(0)
    pl.when(inner_z)(functools.partial(add, 12, 12))
    send_sum(12, 12, 15, when=inner_z)
    pl.when(inner_z)(functools.partial(add, 8, 13))
    send_sum(8, 12, 16, when=inner_z)
    add(4, 9)
    pl.when(inner_z)(functools.partial(add, 4, 16))
    send_sum(4, 4, 14)
    add(0, 8)
    pl.when(inner_z)(functools.partial(add, 0, 15))
    sum_arrived(14)
    total = part[0].astype(jnp.float32) + got[14].astype(jnp.float32)
    out_ref[...] = (hidden_ref[...].astype(jnp.float32) + total).astype(jnp.bfloat16)
    for copy, when in sent:
        if when is None:
            copy.wait_send()
        else:
            pl.when(when)(copy.wait_send)


def dense_body(
    queries,
    key_cache,
    value_cache,
    new_key,
    new_value,
    lengths,
    residual,
    norm_gain,
    expert_ids,
    gate_probs,
    gate_proj,
    up_proj,
    down_proj,
):
    attended = attend(queries, key_cache, value_cache, new_key, new_value, lengths)
    hidden = (residual.astype(jnp.float32) + attended).astype(jnp.bfloat16)
    normed = norm_rows(hidden, norm_gain)
    owners = lax.axis_size("att")
    local_rows, width = hidden.shape
    units = gate_proj.shape[2]
    rest, terms = share_table(expert_ids, gate_probs, owners), []
    for _ in range(3):
        term = lax.reduce_precision(rest, 8, 7)
        terms.append(term.astype(jnp.bfloat16))
        rest = rest - term
    spare = jnp.zeros((local_rows, 128 - 3 * owners), jnp.bfloat16)
    block = jnp.concatenate([normed, *terms, spare], axis=1)
    weight = gate_proj.size + up_proj.size + down_proj.size
    vmem = pl.BlockSpec(memory_space=pltpu.VMEM)
    hbm = pl.BlockSpec(memory_space=pl.ANY)
    return pl.pallas_call(
        expert_kernel,
        out_shape=jax.ShapeDtypeStruct((local_rows, width), jnp.bfloat16),
        in_specs=[vmem, vmem, hbm, hbm, hbm],
        out_specs=vmem,
        scratch_shapes=[
            pltpu.VMEM((owners, local_rows, block.shape[1]), jnp.bfloat16),
            pltpu.VMEM((owners, local_rows, width), jnp.bfloat16),
            pltpu.VMEM((17, local_rows, width), jnp.bfloat16),
            pltpu.VMEM((4 * local_rows, units), jnp.bfloat16),
            pltpu.VMEM((width, units), jnp.bfloat16),
            pltpu.VMEM((width, units), jnp.bfloat16),
            pltpu.VMEM((units, width), jnp.bfloat16),
            pltpu.SemaphoreType.DMA((3,)),
            pltpu.SemaphoreType.DMA((40,)),
            pltpu.SemaphoreType.DMA((16,)),
            pltpu.SemaphoreType.DMA((17,)),
        ],
        compiler_params=pltpu.CompilerParams(
            collective_id=0, has_side_effects=True, vmem_limit_bytes=48 * 1024 * 1024
        ),
        cost_estimate=pl.CostEstimate(
            flops=2 * owners * local_rows * weight,
            bytes_accessed=2 * weight,
            transcendentals=owners * local_rows * units,
        ),
    )(block, hidden, gate_proj[0], up_proj[0], down_proj[0])


def pick_body(*args):
    local_rows, top_count = args[8].shape
    experts_all = lax.axis_size("att") * args[10].shape[0]
    capacity = min(local_rows, max(2, 2 * local_rows * top_count // experts_all))
    dense = lax.axis_size("exp") == 1 and args[10].shape[0] == 1 and capacity == local_rows
    if dense and lax.axis_size("att") == 16:
        return dense_body(*args)
    return body(*args)


def solution(mesh):
    return jax.shard_map(
        pick_body,
        mesh=mesh,
        in_specs=(
            P(("groups", "att"), "exp"),
            P(("groups", "att"), "exp", None, None),
            P(("groups", "att"), "exp", None, None),
            P(("groups", "att"), "exp"),
            P(("groups", "att"), "exp"),
            P(("groups", "att")),
            P(("groups", "att"), "exp"),
            P("exp"),
            P(("groups", "att"), None),
            P(("groups", "att"), None),
            P("att", None, "exp"),
            P("att", None, "exp"),
            P("att", "exp", None),
        ),
        out_specs=P(("groups", "att"), "exp"),
        check_vma=False,
    )
```

```python
import functools
import math

import jax
import jax.numpy as jnp
from jax import lax
from jax.experimental import pallas as pl
from jax.experimental.pallas import tpu as pltpu
from jax.sharding import PartitionSpec as P


def attend(queries, key_cache, value_cache, new_key, new_value, lengths):
    row_count = queries.shape[0]
    groups_kv = key_cache.shape[1]
    head_dim = key_cache.shape[3]
    per_group = queries.shape[1] // (groups_kv * head_dim)
    scaling = 1.0 / math.sqrt(head_dim)
    query_blocks = queries.reshape(row_count, groups_kv, per_group, head_dim)
    cached = (
        jnp.einsum("rghd,rgpd->rghp", query_blocks, key_cache, preferred_element_type=jnp.float32)
        * scaling
    )
    fresh_keys = new_key.reshape(row_count, groups_kv, head_dim)
    own_score = (
        jnp.einsum("rghd,rgd->rgh", query_blocks, fresh_keys, preferred_element_type=jnp.float32)
        * scaling
    )
    position = lax.broadcasted_iota(jnp.int32, cached.shape, 3)
    valid_keys = position < lengths[:, None, None, None]
    cached = jnp.where(valid_keys, cached, -jnp.inf)
    largest = jnp.maximum(jnp.max(cached, axis=3), own_score)
    exp_cached = jnp.exp(cached - largest[..., None])
    own_exp = jnp.exp(own_score - largest)
    denominator = jnp.sum(exp_cached, axis=3) + own_exp
    weights = (exp_cached / denominator[..., None]).astype(jnp.bfloat16)
    own_weight = (own_exp / denominator).astype(jnp.bfloat16)
    fresh_values = new_value.reshape(row_count, groups_kv, head_dim).astype(jnp.float32)
    attended = jnp.einsum(
        "rghp,rgpd->rghd", weights, value_cache, preferred_element_type=jnp.float32
    )
    attended = attended + own_weight.astype(jnp.float32)[..., None] * fresh_values[:, :, None, :]
    return attended.reshape(row_count, per_group * groups_kv * head_dim)


def body(
    queries,
    key_cache,
    value_cache,
    new_key,
    new_value,
    lengths,
    residual,
    norm_gain,
    expert_ids,
    gate_probs,
    gate_proj,
    up_proj,
    down_proj,
):
    attended = attend(queries, key_cache, value_cache, new_key, new_value, lengths)
    hidden = (residual.astype(jnp.float32) + attended).astype(jnp.bfloat16)
    local_rows, top_count = expert_ids.shape
    width_full = down_proj.shape[2]
    owners = lax.axis_size("att")
    local_experts = gate_proj.shape[0]
    experts_all = owners * local_experts
    capacity = min(local_rows, max(2, 2 * local_rows * top_count // experts_all))
    full_rows, full_gain = (
        lax.all_gather(hidden, "exp", axis=1, tiled=True),
        lax.all_gather(norm_gain, "exp", axis=0, tiled=True),
    )
    widened = full_rows.astype(jnp.float32)
    meansq = jnp.sum(widened * widened, axis=1, keepdims=True) / width_full
    normed = (widened * lax.rsqrt(meansq + 1e-06) * full_gain.astype(jnp.float32)[None, :]).astype(
        jnp.bfloat16
    )
    flat_ids = expert_ids.reshape(-1)
    matches = flat_ids[:, None] == flat_ids[None, :]
    earlier = lax.broadcasted_iota(jnp.int32, matches.shape, 1) < lax.broadcasted_iota(
        jnp.int32, matches.shape, 0
    )
    slot_index = jnp.sum((matches & earlier).astype(jnp.int32), axis=1).reshape(
        local_rows, top_count
    )
    target_codes = expert_ids * capacity + slot_index
    targets = lax.broadcasted_iota(jnp.int32, (experts_all * capacity, local_rows, top_count), 0)
    placed = (targets == target_codes[None, :, :]).astype(jnp.float32)
    dispatch = jnp.sum(placed, axis=2).astype(jnp.bfloat16)
    outgoing = jnp.dot(dispatch, normed, preferred_element_type=jnp.float32).astype(jnp.bfloat16)
    outgoing = outgoing.reshape(experts_all, capacity, normed.shape[1])
    arrived = lax.all_to_all(outgoing, "att", split_axis=0, concat_axis=0, tiled=True)
    arrived = arrived.reshape(owners, local_experts, capacity, width_full)
    gate_act = jnp.einsum("secd,edf->secf", arrived, gate_proj, preferred_element_type=jnp.float32)
    up_act = jnp.einsum("secd,edf->secf", arrived, up_proj, preferred_element_type=jnp.float32)
    inner_act = (jax.nn.silu(gate_act) * up_act).astype(jnp.bfloat16)
    partial_out = jnp.einsum(
        "secf,efd->secd", inner_act, down_proj, preferred_element_type=jnp.float32
    )
    returned = lax.psum_scatter(
        partial_out.astype(jnp.bfloat16), "exp", scatter_dimension=3, tiled=True
    )
    returned_rows = lax.all_to_all(returned, "att", split_axis=0, concat_axis=0, tiled=True)
    returned_rows = returned_rows.reshape(experts_all * capacity, returned_rows.shape[3]).astype(
        jnp.float32
    )
    share_norm = gate_probs / jnp.sum(gate_probs, axis=1, keepdims=True)
    combine_table = jnp.sum(placed * share_norm[None, :, :], axis=2)
    combined = jnp.dot(combine_table.T, returned_rows, precision=lax.Precision.HIGHEST)
    return (hidden.astype(jnp.float32) + combined).astype(jnp.bfloat16)


def norm_rows(hidden, norm_gain):
    widened = hidden.astype(jnp.float32)
    meansq = jnp.sum(widened * widened, axis=1, keepdims=True) / hidden.shape[1]
    return (widened * lax.rsqrt(meansq + 1e-06) * norm_gain.astype(jnp.float32)[None, :]).astype(
        jnp.bfloat16
    )


def share_table(expert_ids, gate_probs, experts_all):
    share_norm = gate_probs / jnp.sum(gate_probs, axis=1, keepdims=True)
    hits = expert_ids[:, :, None] == jnp.arange(experts_all, dtype=jnp.int32)[None, None, :]
    return jnp.sum(jnp.where(hits, share_norm[:, :, None], 0.0), axis=1)


def expert_kernel(
    block_ref,
    hidden_ref,
    gate_hbm,
    up_hbm,
    down_hbm,
    out_ref,
    rows,
    part,
    got,
    inner,
    gate,
    up,
    down,
    weight_sem,
    send_sem,
    row_recv,
    sum_recv,
):
    me = lax.axis_index("att")
    layer = lax.div(me, 4)
    inner_z = (layer == 1) | (layer == 2)
    partners = {m: me + m - 2 * m * (lax.div(me, m) % 2) for m in (1, 2, 4)}
    partners[12] = me + 4 * (3 - 2 * layer)
    block_rows, width = hidden_ref.shape

    barrier = pltpu.get_barrier_semaphore()
    for m in (1, 2, 4, 12):
        pl.semaphore_signal(
            barrier, inc=1, device_id={"att": partners[m]}, device_id_type=pl.DeviceIdType.MESH
        )
    loads = [
        pltpu.make_async_copy(source, held, weight_sem.at[i])
        for i, (source, held) in enumerate(((gate_hbm, gate), (up_hbm, up), (down_hbm, down)))
    ]
    for load in loads:
        load.start()
    pl.semaphore_wait(barrier, 4)

    sent = []

    def start(copy, when):
        sent.append((copy, when))
        if when is None:
            copy.start()
        else:
            pl.when(when)(copy.start)

    def forward(slot, *masks, when=None):
        for m in masks:
            copy = pltpu.make_async_remote_copy(
                src_ref=block_ref if slot == 0 else rows.at[slot],
                dst_ref=rows.at[slot ^ m],
                send_sem=send_sem.at[len(sent)],
                recv_sem=row_recv.at[slot ^ m],
                device_id={"att": partners[m]},
                device_id_type=pl.DeviceIdType.MESH,
            )
            start(copy, when)

    def arrived(*slots):
        for slot in slots:
            pltpu.make_async_remote_copy(
                src_ref=rows.at[slot],
                dst_ref=rows.at[slot],
                send_sem=row_recv.at[slot],
                recv_sem=row_recv.at[slot],
                device_id={"att": partners[1]},
                device_id_type=pl.DeviceIdType.MESH,
            ).wait_recv()

    half = block_rows // 2

    def piece(ref, index, h):
        return ref.at[index, h * half : (h + 1) * half]

    def send_sum(slot, m, place, h, when=None):
        copy = pltpu.make_async_remote_copy(
            src_ref=piece(part, slot, h),
            dst_ref=piece(got, place, h),
            send_sem=send_sem.at[len(sent)],
            recv_sem=sum_recv.at[2 * place + h],
            device_id={"att": partners[m]},
            device_id_type=pl.DeviceIdType.MESH,
        )
        start(copy, when)

    def sum_arrived(place, h):
        pltpu.make_async_remote_copy(
            src_ref=piece(got, place, h),
            dst_ref=piece(got, place, h),
            send_sem=sum_recv.at[2 * place + h],
            recv_sem=sum_recv.at[2 * place + h],
            device_id={"att": partners[1]},
            device_id_type=pl.DeviceIdType.MESH,
        ).wait_recv()

    def add(slot, place, h):
        sum_arrived(place, h)
        held, came = piece(part, slot, h), piece(got, place, h)
        held[...] = (held[...].astype(jnp.float32) + came[...].astype(jnp.float32)).astype(
            jnp.bfloat16
        )

    def experts(chunk):
        first, count = 4 * chunk, 4
        length = count * block_rows

        def hidden_step(j, carry):
            columns = pl.ds(pl.multiple_of(j * 256, 256), 256)
            held = rows[first : first + count, :, :width].reshape(length, width)
            g = jnp.dot(held, gate[:, columns], preferred_element_type=jnp.float32)
            u = jnp.dot(held, up[:, columns], preferred_element_type=jnp.float32)
            inner[:, columns] = (g / (1.0 + jnp.exp(-g)) * u).astype(jnp.bfloat16)
            return carry

        lax.fori_loop(0, gate.shape[1] // 256, hidden_step, 0)
        pieces = rows[first : first + count, :, width:].reshape(length, 128).astype(jnp.float32)
        lane = lax.broadcasted_iota(jnp.int32, pieces.shape, 1)
        mine = (lane == me) | (lane == me + 16) | (lane == me + 32)
        share = jnp.sum(jnp.where(mine, pieces, 0.0), axis=1, keepdims=True)

        def out_step(j, carry):
            columns = pl.ds(pl.multiple_of(j * 512, 512), 512)
            o = jnp.dot(inner[...], down[:, columns], preferred_element_type=jnp.float32)
            o = (o.astype(jnp.bfloat16).astype(jnp.float32) * share).astype(jnp.bfloat16)
            part[first : first + count, :, columns] = o.reshape(count, block_rows, 512)
            return carry

        lax.fori_loop(0, width // 512, out_step, 0)
        for xr in (1, 0):
            for h in (0, 1):
                send_sum(first + 2 * xr + 1, 1, 2 * chunk + xr, h)

    def across_x(chunk):
        for h in (0, 1):
            add(4 * chunk + 2, 2 * chunk + 1, h)
            send_sum(4 * chunk + 2, 2, 8 + chunk, h)
        for h in (0, 1):
            add(4 * chunk, 2 * chunk, h)

    def inner_add(slot, place, h):
        pl.when(inner_z)(functools.partial(add, slot, place, h))

    outer_z = jnp.logical_not(inner_z)
    forward(0, 2, 4)
    forward(0, 12, when=inner_z)
    forward(0, 1)
    rows[0] = block_ref[...]
    arrived(4)
    forward(4, 2)
    forward(4, 12, when=inner_z)
    forward(4, 1)
    pl.when(inner_z)(functools.partial(arrived, 12))
    forward(12, 4, when=inner_z)
    arrived(2)
    forward(2, 1)
    for load in loads:
        load.wait()
    arrived(1, 3)
    experts(0)
    arrived(8)
    forward(8, 2)
    forward(8, 4, when=inner_z)
    forward(8, 1)
    arrived(6)
    forward(6, 1)
    arrived(5, 7)
    experts(1)
    pl.when(outer_z)(functools.partial(arrived, 12))
    forward(12, 2, 1)
    arrived(10)
    forward(10, 1)
    arrived(9, 11)
    experts(2)
    across_x(2)
    arrived(14)
    forward(14, 1)
    arrived(13, 15)
    experts(3)
    across_x(3)
    for h in (0, 1):
        add(8, 10, h)
        send_sum(8, 4, 12, h, when=outer_z)
    add(12, 11, 0)
    send_sum(12, 4, 13, 0, when=outer_z)
    across_x(1)
    add(12, 11, 1)
    send_sum(12, 4, 13, 1, when=outer_z)
    for h in (0, 1):
        inner_add(12, 12, h)
        send_sum(12, 12, 15, h, when=inner_z)
    across_x(0)
    for h in (0, 1):
        inner_add(8, 13, h)
        send_sum(8, 12, 16, h, when=inner_z)
    for h in (0, 1):
        add(4, 9, h)
        inner_add(4, 16, h)
        send_sum(4, 4, 14, h)
    for h in (0, 1):
        add(0, 8, h)
        inner_add(0, 15, h)
    for h in (0, 1):
        sum_arrived(14, h)
        span = slice(h * half, (h + 1) * half)
        total = part[0, span].astype(jnp.float32) + got[14, span].astype(jnp.float32)
        out_ref[span] = (hidden_ref[span].astype(jnp.float32) + total).astype(jnp.bfloat16)
    for copy, when in sent:
        if when is None:
            copy.wait_send()
        else:
            pl.when(when)(copy.wait_send)


def dense_body(
    queries,
    key_cache,
    value_cache,
    new_key,
    new_value,
    lengths,
    residual,
    norm_gain,
    expert_ids,
    gate_probs,
    gate_proj,
    up_proj,
    down_proj,
):
    attended = attend(queries, key_cache, value_cache, new_key, new_value, lengths)
    hidden = (residual.astype(jnp.float32) + attended).astype(jnp.bfloat16)
    normed = norm_rows(hidden, norm_gain)
    owners = lax.axis_size("att")
    local_rows, width = hidden.shape
    units = gate_proj.shape[2]
    rest, terms = share_table(expert_ids, gate_probs, owners), []
    for _ in range(3):
        term = lax.reduce_precision(rest, 8, 7)
        terms.append(term.astype(jnp.bfloat16))
        rest = rest - term
    spare = jnp.zeros((local_rows, 128 - 3 * owners), jnp.bfloat16)
    block = jnp.concatenate([normed, *terms, spare], axis=1)
    weight = gate_proj.size + up_proj.size + down_proj.size
    vmem = pl.BlockSpec(memory_space=pltpu.VMEM)
    hbm = pl.BlockSpec(memory_space=pl.ANY)
    return pl.pallas_call(
        expert_kernel,
        out_shape=jax.ShapeDtypeStruct((local_rows, width), jnp.bfloat16),
        in_specs=[vmem, vmem, hbm, hbm, hbm],
        out_specs=vmem,
        scratch_shapes=[
            pltpu.VMEM((owners, local_rows, block.shape[1]), jnp.bfloat16),
            pltpu.VMEM((owners, local_rows, width), jnp.bfloat16),
            pltpu.VMEM((17, local_rows, width), jnp.bfloat16),
            pltpu.VMEM((4 * local_rows, units), jnp.bfloat16),
            pltpu.VMEM((width, units), jnp.bfloat16),
            pltpu.VMEM((width, units), jnp.bfloat16),
            pltpu.VMEM((units, width), jnp.bfloat16),
            pltpu.SemaphoreType.DMA((3,)),
            pltpu.SemaphoreType.DMA((64,)),
            pltpu.SemaphoreType.DMA((16,)),
            pltpu.SemaphoreType.DMA((34,)),
        ],
        compiler_params=pltpu.CompilerParams(
            collective_id=0, has_side_effects=True, vmem_limit_bytes=48 * 1024 * 1024
        ),
        cost_estimate=pl.CostEstimate(
            flops=2 * owners * local_rows * weight,
            bytes_accessed=2 * weight,
            transcendentals=owners * local_rows * units,
        ),
    )(block, hidden, gate_proj[0], up_proj[0], down_proj[0])


def pick_body(*args):
    local_rows, top_count = args[8].shape
    experts_all = lax.axis_size("att") * args[10].shape[0]
    capacity = min(local_rows, max(2, 2 * local_rows * top_count // experts_all))
    dense = lax.axis_size("exp") == 1 and args[10].shape[0] == 1 and capacity == local_rows
    if dense and lax.axis_size("att") == 16:
        return dense_body(*args)
    return body(*args)


def solution(mesh):
    return jax.shard_map(
        pick_body,
        mesh=mesh,
        in_specs=(
            P(("groups", "att"), "exp"),
            P(("groups", "att"), "exp", None, None),
            P(("groups", "att"), "exp", None, None),
            P(("groups", "att"), "exp"),
            P(("groups", "att"), "exp"),
            P(("groups", "att")),
            P(("groups", "att"), "exp"),
            P("exp"),
            P(("groups", "att"), None),
            P(("groups", "att"), None),
            P("att", None, "exp"),
            P("att", None, "exp"),
            P("att", "exp", None),
        ),
        out_specs=P(("groups", "att"), "exp"),
        check_vma=False,
    )
```

```python
import functools
import math

import jax
import jax.numpy as jnp
from jax import lax
from jax.experimental import pallas as pl
from jax.experimental.pallas import tpu as pltpu
from jax.sharding import PartitionSpec as P


def attend(queries, key_cache, value_cache, new_key, new_value, lengths):
    row_count = queries.shape[0]
    groups_kv = key_cache.shape[1]
    head_dim = key_cache.shape[3]
    per_group = queries.shape[1] // (groups_kv * head_dim)
    scaling = 1.0 / math.sqrt(head_dim)
    query_blocks = queries.reshape(row_count, groups_kv, per_group, head_dim)
    cached = (
        jnp.einsum("rghd,rgpd->rghp", query_blocks, key_cache, preferred_element_type=jnp.float32)
        * scaling
    )
    fresh_keys = new_key.reshape(row_count, groups_kv, head_dim)
    own_score = (
        jnp.einsum("rghd,rgd->rgh", query_blocks, fresh_keys, preferred_element_type=jnp.float32)
        * scaling
    )
    position = lax.broadcasted_iota(jnp.int32, cached.shape, 3)
    valid_keys = position < lengths[:, None, None, None]
    cached = jnp.where(valid_keys, cached, -jnp.inf)
    largest = jnp.maximum(jnp.max(cached, axis=3), own_score)
    exp_cached = jnp.exp(cached - largest[..., None])
    own_exp = jnp.exp(own_score - largest)
    denominator = jnp.sum(exp_cached, axis=3) + own_exp
    weights = (exp_cached / denominator[..., None]).astype(jnp.bfloat16)
    own_weight = (own_exp / denominator).astype(jnp.bfloat16)
    fresh_values = new_value.reshape(row_count, groups_kv, head_dim).astype(jnp.float32)
    attended = jnp.einsum(
        "rghp,rgpd->rghd", weights, value_cache, preferred_element_type=jnp.float32
    )
    attended = attended + own_weight.astype(jnp.float32)[..., None] * fresh_values[:, :, None, :]
    return attended.reshape(row_count, per_group * groups_kv * head_dim)


def body(
    queries,
    key_cache,
    value_cache,
    new_key,
    new_value,
    lengths,
    residual,
    norm_gain,
    expert_ids,
    gate_probs,
    gate_proj,
    up_proj,
    down_proj,
):
    attended = attend(queries, key_cache, value_cache, new_key, new_value, lengths)
    hidden = (residual.astype(jnp.float32) + attended).astype(jnp.bfloat16)
    local_rows, top_count = expert_ids.shape
    width_full = down_proj.shape[2]
    owners = lax.axis_size("att")
    local_experts = gate_proj.shape[0]
    experts_all = owners * local_experts
    capacity = min(local_rows, max(2, 2 * local_rows * top_count // experts_all))
    full_rows, full_gain = (
        lax.all_gather(hidden, "exp", axis=1, tiled=True),
        lax.all_gather(norm_gain, "exp", axis=0, tiled=True),
    )
    widened = full_rows.astype(jnp.float32)
    meansq = jnp.sum(widened * widened, axis=1, keepdims=True) / width_full
    normed = (widened * lax.rsqrt(meansq + 1e-06) * full_gain.astype(jnp.float32)[None, :]).astype(
        jnp.bfloat16
    )
    flat_ids = expert_ids.reshape(-1)
    matches = flat_ids[:, None] == flat_ids[None, :]
    earlier = lax.broadcasted_iota(jnp.int32, matches.shape, 1) < lax.broadcasted_iota(
        jnp.int32, matches.shape, 0
    )
    slot_index = jnp.sum((matches & earlier).astype(jnp.int32), axis=1).reshape(
        local_rows, top_count
    )
    target_codes = expert_ids * capacity + slot_index
    targets = lax.broadcasted_iota(jnp.int32, (experts_all * capacity, local_rows, top_count), 0)
    placed = (targets == target_codes[None, :, :]).astype(jnp.float32)
    dispatch = jnp.sum(placed, axis=2).astype(jnp.bfloat16)
    outgoing = jnp.dot(dispatch, normed, preferred_element_type=jnp.float32).astype(jnp.bfloat16)
    outgoing = outgoing.reshape(experts_all, capacity, normed.shape[1])
    arrived = lax.all_to_all(outgoing, "att", split_axis=0, concat_axis=0, tiled=True)
    arrived = arrived.reshape(owners, local_experts, capacity, width_full)
    gate_act = jnp.einsum("secd,edf->secf", arrived, gate_proj, preferred_element_type=jnp.float32)
    up_act = jnp.einsum("secd,edf->secf", arrived, up_proj, preferred_element_type=jnp.float32)
    inner_act = (jax.nn.silu(gate_act) * up_act).astype(jnp.bfloat16)
    partial_out = jnp.einsum(
        "secf,efd->secd", inner_act, down_proj, preferred_element_type=jnp.float32
    )
    returned = lax.psum_scatter(
        partial_out.astype(jnp.bfloat16), "exp", scatter_dimension=3, tiled=True
    )
    returned_rows = lax.all_to_all(returned, "att", split_axis=0, concat_axis=0, tiled=True)
    returned_rows = returned_rows.reshape(experts_all * capacity, returned_rows.shape[3]).astype(
        jnp.float32
    )
    share_norm = gate_probs / jnp.sum(gate_probs, axis=1, keepdims=True)
    combine_table = jnp.sum(placed * share_norm[None, :, :], axis=2)
    combined = jnp.dot(combine_table.T, returned_rows, precision=lax.Precision.HIGHEST)
    return (hidden.astype(jnp.float32) + combined).astype(jnp.bfloat16)


def norm_rows(hidden, norm_gain):
    widened = hidden.astype(jnp.float32)
    meansq = jnp.sum(widened * widened, axis=1, keepdims=True) / hidden.shape[1]
    return (widened * lax.rsqrt(meansq + 1e-06) * norm_gain.astype(jnp.float32)[None, :]).astype(
        jnp.bfloat16
    )


def share_table(expert_ids, gate_probs, experts_all):
    share_norm = gate_probs / jnp.sum(gate_probs, axis=1, keepdims=True)
    hits = expert_ids[:, :, None] == jnp.arange(experts_all, dtype=jnp.int32)[None, None, :]
    return jnp.sum(jnp.where(hits, share_norm[:, :, None], 0.0), axis=1)


def expert_kernel(
    block_ref,
    hidden_ref,
    gate_hbm,
    up_hbm,
    down_hbm,
    out_ref,
    rows,
    part,
    got,
    inner,
    gate,
    up,
    down,
    weight_sem,
    send_sem,
    row_recv,
    sum_recv,
):
    me = lax.axis_index("att")
    layer = lax.div(me, 4)
    inner_z = (layer == 1) | (layer == 2)
    partners = {m: me + m - 2 * m * (lax.div(me, m) % 2) for m in (1, 2, 4)}
    partners[12] = me + 4 * (3 - 2 * layer)
    block_rows, width = hidden_ref.shape

    barrier = pltpu.get_barrier_semaphore()
    for m in (1, 2, 4, 12):
        pl.semaphore_signal(
            barrier, inc=1, device_id={"att": partners[m]}, device_id_type=pl.DeviceIdType.MESH
        )
    loads = [
        pltpu.make_async_copy(source, held, weight_sem.at[i])
        for i, (source, held) in enumerate(((gate_hbm, gate), (up_hbm, up), (down_hbm, down)))
    ]
    for load in loads:
        load.start()
    pl.semaphore_wait(barrier, 4)

    sent = []

    def start(copy, when):
        sent.append((copy, when))
        if when is None:
            copy.start()
        else:
            pl.when(when)(copy.start)

    def forward(slot, *masks, when=None):
        for m in masks:
            copy = pltpu.make_async_remote_copy(
                src_ref=block_ref if slot == 0 else rows.at[slot],
                dst_ref=rows.at[slot ^ m],
                send_sem=send_sem.at[len(sent)],
                recv_sem=row_recv.at[slot ^ m],
                device_id={"att": partners[m]},
                device_id_type=pl.DeviceIdType.MESH,
            )
            start(copy, when)

    def arrived(*slots):
        for slot in slots:
            pltpu.make_async_remote_copy(
                src_ref=rows.at[slot],
                dst_ref=rows.at[slot],
                send_sem=row_recv.at[slot],
                recv_sem=row_recv.at[slot],
                device_id={"att": partners[1]},
                device_id_type=pl.DeviceIdType.MESH,
            ).wait_recv()

    half = block_rows // 2

    def piece(ref, index, h):
        return ref.at[index, h * half : (h + 1) * half]

    def send_sum(slot, m, place, h, when=None):
        copy = pltpu.make_async_remote_copy(
            src_ref=piece(part, slot, h),
            dst_ref=piece(got, place, h),
            send_sem=send_sem.at[len(sent)],
            recv_sem=sum_recv.at[2 * place + h],
            device_id={"att": partners[m]},
            device_id_type=pl.DeviceIdType.MESH,
        )
        start(copy, when)

    def sum_arrived(place, h):
        pltpu.make_async_remote_copy(
            src_ref=piece(got, place, h),
            dst_ref=piece(got, place, h),
            send_sem=sum_recv.at[2 * place + h],
            recv_sem=sum_recv.at[2 * place + h],
            device_id={"att": partners[1]},
            device_id_type=pl.DeviceIdType.MESH,
        ).wait_recv()

    def add(slot, place, h):
        sum_arrived(place, h)
        held, came = piece(part, slot, h), piece(got, place, h)
        held[...] = (held[...].astype(jnp.float32) + came[...].astype(jnp.float32)).astype(
            jnp.bfloat16
        )

    def experts(chunk):
        first, count = 4 * chunk, 4
        length = count * block_rows

        def hidden_step(j, carry):
            columns = pl.ds(pl.multiple_of(j * 256, 256), 256)
            held = rows[first : first + count, :, :width].reshape(length, width)
            g = jnp.dot(held, gate[:, columns], preferred_element_type=jnp.float32)
            u = jnp.dot(held, up[:, columns], preferred_element_type=jnp.float32)
            inner[:, columns] = (g / (1.0 + jnp.exp(-g)) * u).astype(jnp.bfloat16)
            return carry

        lax.fori_loop(0, gate.shape[1] // 256, hidden_step, 0)
        pieces = rows[first : first + count, :, width:].reshape(length, 128).astype(jnp.float32)
        lane = lax.broadcasted_iota(jnp.int32, pieces.shape, 1)
        mine = (lane == me) | (lane == me + 16) | (lane == me + 32)
        share = jnp.sum(jnp.where(mine, pieces, 0.0), axis=1, keepdims=True)

        def out_step(j, carry):
            columns = pl.ds(pl.multiple_of(j * 512, 512), 512)
            o = jnp.dot(inner[...], down[:, columns], preferred_element_type=jnp.float32)
            o = (o.astype(jnp.bfloat16).astype(jnp.float32) * share).astype(jnp.bfloat16)
            part[first : first + count, :, columns] = o.reshape(count, block_rows, 512)
            return carry

        lax.fori_loop(0, width // 512, out_step, 0)
        for xr in (1, 0):
            for h in (0, 1):
                send_sum(first + 2 * xr + 1, 1, 2 * chunk + xr, h)

    def across_x(chunk):
        for h in (0, 1):
            add(4 * chunk + 2, 2 * chunk + 1, h)
            send_sum(4 * chunk + 2, 2, 8 + chunk, h)
        for h in (0, 1):
            add(4 * chunk, 2 * chunk, h)

    def inner_add(slot, place, h):
        pl.when(inner_z)(functools.partial(add, slot, place, h))

    outer_z = jnp.logical_not(inner_z)
    forward(0, 2, 4)
    forward(0, 12, when=inner_z)
    forward(0, 1)
    rows[0] = block_ref[...]
    arrived(4)
    forward(4, 2)
    forward(4, 12, when=inner_z)
    forward(4, 1)
    pl.when(inner_z)(functools.partial(arrived, 12))
    forward(12, 4, when=inner_z)
    arrived(2)
    forward(2, 1)
    for load in loads:
        load.wait()
    arrived(1, 3)
    experts(0)
    arrived(8)
    forward(8, 2)
    forward(8, 4, when=inner_z)
    forward(8, 1)
    arrived(6)
    forward(6, 1)
    arrived(5, 7)
    experts(1)
    pl.when(outer_z)(functools.partial(arrived, 12))
    forward(12, 2, 1)
    arrived(10)
    forward(10, 1)
    arrived(9, 11)
    experts(2)
    arrived(14)
    forward(14, 1)
    across_x(2)
    arrived(13, 15)
    experts(3)
    across_x(3)
    for h in (0, 1):
        add(8, 10, h)
        send_sum(8, 4, 12, h, when=outer_z)
    add(12, 11, 0)
    send_sum(12, 4, 13, 0, when=outer_z)
    across_x(1)
    add(12, 11, 1)
    send_sum(12, 4, 13, 1, when=outer_z)
    for h in (0, 1):
        inner_add(12, 12, h)
        send_sum(12, 12, 15, h, when=inner_z)
    across_x(0)
    for h in (0, 1):
        inner_add(8, 13, h)
        send_sum(8, 12, 16, h, when=inner_z)
    for h in (0, 1):
        add(4, 9, h)
        inner_add(4, 16, h)
        send_sum(4, 4, 14, h)
    for h in (0, 1):
        add(0, 8, h)
        inner_add(0, 15, h)
    for h in (0, 1):
        sum_arrived(14, h)
        span = slice(h * half, (h + 1) * half)
        total = part[0, span].astype(jnp.float32) + got[14, span].astype(jnp.float32)
        out_ref[span] = (hidden_ref[span].astype(jnp.float32) + total).astype(jnp.bfloat16)
    for copy, when in sent:
        if when is None:
            copy.wait_send()
        else:
            pl.when(when)(copy.wait_send)


def dense_body(
    queries,
    key_cache,
    value_cache,
    new_key,
    new_value,
    lengths,
    residual,
    norm_gain,
    expert_ids,
    gate_probs,
    gate_proj,
    up_proj,
    down_proj,
):
    attended = attend(queries, key_cache, value_cache, new_key, new_value, lengths)
    hidden = (residual.astype(jnp.float32) + attended).astype(jnp.bfloat16)
    normed = norm_rows(hidden, norm_gain)
    owners = lax.axis_size("att")
    local_rows, width = hidden.shape
    units = gate_proj.shape[2]
    rest, terms = share_table(expert_ids, gate_probs, owners), []
    for _ in range(3):
        term = lax.reduce_precision(rest, 8, 7)
        terms.append(term.astype(jnp.bfloat16))
        rest = rest - term
    spare = jnp.zeros((local_rows, 128 - 3 * owners), jnp.bfloat16)
    block = jnp.concatenate([normed, *terms, spare], axis=1)
    weight = gate_proj.size + up_proj.size + down_proj.size
    vmem = pl.BlockSpec(memory_space=pltpu.VMEM)
    hbm = pl.BlockSpec(memory_space=pl.ANY)
    return pl.pallas_call(
        expert_kernel,
        out_shape=jax.ShapeDtypeStruct((local_rows, width), jnp.bfloat16),
        in_specs=[vmem, vmem, hbm, hbm, hbm],
        out_specs=vmem,
        scratch_shapes=[
            pltpu.VMEM((owners, local_rows, block.shape[1]), jnp.bfloat16),
            pltpu.VMEM((owners, local_rows, width), jnp.bfloat16),
            pltpu.VMEM((17, local_rows, width), jnp.bfloat16),
            pltpu.VMEM((4 * local_rows, units), jnp.bfloat16),
            pltpu.VMEM((width, units), jnp.bfloat16),
            pltpu.VMEM((width, units), jnp.bfloat16),
            pltpu.VMEM((units, width), jnp.bfloat16),
            pltpu.SemaphoreType.DMA((3,)),
            pltpu.SemaphoreType.DMA((64,)),
            pltpu.SemaphoreType.DMA((16,)),
            pltpu.SemaphoreType.DMA((34,)),
        ],
        compiler_params=pltpu.CompilerParams(
            collective_id=0, has_side_effects=True, vmem_limit_bytes=48 * 1024 * 1024
        ),
        cost_estimate=pl.CostEstimate(
            flops=2 * owners * local_rows * weight,
            bytes_accessed=2 * weight,
            transcendentals=owners * local_rows * units,
        ),
    )(block, hidden, gate_proj[0], up_proj[0], down_proj[0])


def pick_body(*args):
    local_rows, top_count = args[8].shape
    experts_all = lax.axis_size("att") * args[10].shape[0]
    capacity = min(local_rows, max(2, 2 * local_rows * top_count // experts_all))
    dense = lax.axis_size("exp") == 1 and args[10].shape[0] == 1 and capacity == local_rows
    if dense and lax.axis_size("att") == 16:
        return dense_body(*args)
    return body(*args)


def solution(mesh):
    return jax.shard_map(
        pick_body,
        mesh=mesh,
        in_specs=(
            P(("groups", "att"), "exp"),
            P(("groups", "att"), "exp", None, None),
            P(("groups", "att"), "exp", None, None),
            P(("groups", "att"), "exp"),
            P(("groups", "att"), "exp"),
            P(("groups", "att")),
            P(("groups", "att"), "exp"),
            P("exp"),
            P(("groups", "att"), None),
            P(("groups", "att"), None),
            P("att", None, "exp"),
            P("att", None, "exp"),
            P("att", "exp", None),
        ),
        out_specs=P(("groups", "att"), "exp"),
        check_vma=False,
    )
```
